32 devices in a mesh: groups: 2 (over x), tensor: 16 (over z, y, core).
Axes of the slice: x: 2, y: 2, z: 4, core: 2. Of those that a mesh axis runs over, the one named last changes fastest.
Arguments:
- rows_in: bfloat16 [128, 5120], P(('groups', 'tensor')), parts along dimension 0, may hold values from -6 to 6
- grad_out: bfloat16 [128, 5120], P(('groups', 'tensor')), parts along dimension 0, may hold values from -6 to 6
- w_gate: bfloat16 [5120, 25600], P(None, 'tensor'), may hold values from -0.078125 to 0.078125
- w_up: bfloat16 [5120, 25600], P(None, 'tensor'), may hold values from -0.078125 to 0.078125
- w_down: bfloat16 [25600, 5120], P('tensor'), may hold values from -0.0390625 to 0.0390625
- a_gate: bfloat16 [5120, 64], P('tensor'), may hold values from -0.078125 to 0.078125
- b_gate: bfloat16 [64, 25600], P(None, 'tensor'), may hold values from -0.75 to 0.75
- a_up: bfloat16 [5120, 64], P('tensor'), may hold values from -0.078125 to 0.078125
- b_up: bfloat16 [64, 25600], P(None, 'tensor'), may hold values from -0.75 to 0.75
- a_down: bfloat16 [25600, 64], P('tensor'), may hold values from -0.0390625 to 0.0390625
- b_down: bfloat16 [64, 5120], P(None, 'tensor'), may hold values from -0.75 to 0.75
Outputs:
- grad_rows: float32 [128, 5120], P(('groups', 'tensor')), parts along dimension 0
- grad_a_gate: float32 [10240, 64], P(('groups', 'tensor')), parts along dimension 0
- grad_b_gate: float32 [128, 25600], P('groups', 'tensor'), parts along dimension 0
- grad_a_up: float32 [10240, 64], P(('groups', 'tensor')), parts along dimension 0
- grad_b_up: float32 [128, 25600], P('groups', 'tensor'), parts along dimension 0
- grad_a_down: float32 [51200, 64], P(('groups', 'tensor')), parts along dimension 0
- grad_b_down: float32 [128, 5120], P('groups', 'tensor'), parts along dimension 0
The draws below stay inside these ranges and needn't reach their ends.
There are 2 independent parts, one for each index of `groups`. The reference program is written for one: setup_inputs(seed, part) draws one part's arguments, and reference() takes and returns one part's arrays. A program takes and returns all parts, laid end to end along the dimension named above; an argument that names none is the same for every part. Nothing has to cross between parts.
All inputs are finite; a program needn't handle non-finite values.
Results may differ from the reference program's by a relative error of at most 0.0055.
Values may be sent and summed in bfloat16 or wider, within the bound.
No kernel may reach another device: no remote copies, remote signals or barrier semaphores. Data moves between devices by JAX's collectives and lax.ppermute only.
A program may use at most 128 MiB of HBM per device.

```python
import jax
import jax.numpy as jnp
from jax import lax

D = 5120
FF = 25600
RANK = 64
ROWS = 64


def shard_levels(key, shape, cuts, smallest, largest):
    loudness, own = 1.0, jax.random.fold_in(key, 6)
    for position, shards_of in cuts:
        heights = jnp.exp(jax.random.uniform(jax.random.fold_in(own, position), (shards_of,), jnp.float32, smallest / len(cuts), largest / len(cuts)))
        loudness = loudness * jnp.repeat(heights, shape[position] // shards_of).reshape([-1 if axis == position else 1 for axis in range(len(shape))])
    return loudness


def normal_values(rng, shape, spread, limit, split=(), kind=jnp.bfloat16):
    gain = shard_levels(rng, shape, split, -0.22, 0.18) if split else 1.0
    array = jax.random.normal(rng, shape, jnp.float32) * spread * gain
    return jnp.minimum(jnp.maximum(array, -limit), limit).astype(kind)


def setup_inputs(seed: int = 0, part: int = 0) -> dict:
    arg_keys = jax.random.split(jax.random.key(seed), 12)
    own_keys = jax.random.split(jax.random.fold_in(arg_keys[11], part), 12)
    rows_in = normal_values(own_keys[0], (ROWS, D), 1.0, 6.0, ((0, 16),))
    grad_out = normal_values(own_keys[1], (ROWS, D), 1.0, 6.0, ((0, 16),))
    w_gate = normal_values(arg_keys[2], (D, FF), D ** -0.5, 0.078125, ((1, 16),))
    w_up = normal_values(arg_keys[3], (D, FF), D ** -0.5, 0.078125, ((1, 16),))
    w_down = normal_values(arg_keys[4], (FF, D), FF ** -0.5, 0.0390625, ((0, 16),))
    a_gate = normal_values(arg_keys[5], (D, RANK), D ** -0.5, 0.078125, ((0, 16),))
    b_gate = normal_values(arg_keys[6], (RANK, FF), RANK ** -0.5, 0.75, ((1, 16),))
    a_up = normal_values(arg_keys[7], (D, RANK), D ** -0.5, 0.078125, ((0, 16),))
    b_up = normal_values(arg_keys[8], (RANK, FF), RANK ** -0.5, 0.75, ((1, 16),))
    a_down = normal_values(arg_keys[9], (FF, RANK), FF ** -0.5, 0.0390625, ((0, 16),))
    b_down = normal_values(arg_keys[10], (RANK, D), RANK ** -0.5, 0.75, ((1, 16),))
    return dict(rows_in=rows_in, grad_out=grad_out, w_gate=w_gate, w_up=w_up, w_down=w_down, a_gate=a_gate, b_gate=b_gate, a_up=a_up, b_up=b_up, a_down=a_down, b_down=b_down)


def reference(rows_in, grad_out, w_gate, w_up, w_down, a_gate, b_gate, a_up, b_up, a_down, b_down):
    high = lax.Precision.HIGHEST
    lat_gate = jnp.dot(rows_in, a_gate, preferred_element_type=jnp.float32).astype(jnp.bfloat16)
    lat_up = jnp.dot(rows_in, a_up, preferred_element_type=jnp.float32).astype(jnp.bfloat16)
    gate_pre = jnp.dot(rows_in, w_gate, preferred_element_type=jnp.float32) + jnp.dot(lat_gate, b_gate, preferred_element_type=jnp.float32)
    up_pre = jnp.dot(rows_in, w_up, preferred_element_type=jnp.float32) + jnp.dot(lat_up, b_up, preferred_element_type=jnp.float32)
    sigma = jax.nn.sigmoid(gate_pre)
    act = gate_pre * sigma
    hidden = (act * up_pre).astype(jnp.bfloat16)
    lat_down = jnp.dot(hidden, a_down, preferred_element_type=jnp.float32).astype(jnp.bfloat16)
    grad_b_down = jnp.dot(lat_down.T, grad_out, preferred_element_type=jnp.float32)
    back = jnp.dot(grad_out, b_down.T, preferred_element_type=jnp.float32).astype(jnp.bfloat16)
    grad_hidden = jnp.dot(grad_out, w_down.T, preferred_element_type=jnp.float32) + jnp.dot(back, a_down.T, preferred_element_type=jnp.float32)
    grad_a_down = jnp.dot(hidden.T, back, preferred_element_type=jnp.float32)
    d_up = (grad_hidden * act).astype(jnp.bfloat16)
    d_gate = (grad_hidden * up_pre * sigma * (1.0 + gate_pre * (1.0 - sigma))).astype(jnp.bfloat16)
    grad_b_up = jnp.dot(lat_up.T, d_up, preferred_element_type=jnp.float32)
    grad_b_gate = jnp.dot(lat_gate.T, d_gate, preferred_element_type=jnp.float32)
    t_up = jnp.dot(d_up, b_up.T, preferred_element_type=jnp.float32)
    t_gate = jnp.dot(d_gate, b_gate.T, preferred_element_type=jnp.float32)
    rows_float = rows_in.astype(jnp.float32)
    grad_a_up = jnp.dot(rows_float.T, t_up, precision=high)
    grad_a_gate = jnp.dot(rows_float.T, t_gate, precision=high)
    grad_rows = jnp.dot(d_gate, w_gate.T, preferred_element_type=jnp.float32) + jnp.dot(d_up, w_up.T, preferred_element_type=jnp.float32)
    grad_rows = grad_rows + jnp.dot(t_gate, a_gate.astype(jnp.float32).T, precision=high) + jnp.dot(t_up, a_up.astype(jnp.float32).T, precision=high)
    return grad_rows, grad_a_gate, grad_b_gate, grad_a_up, grad_b_up, grad_a_down, grad_b_down
```

```python
import jax
import jax.numpy as jnp
from jax import lax
from jax.sharding import PartitionSpec as P


def dot(left, right):
    return jnp.dot(left, right, preferred_element_type=jnp.float32)


def halves(values):
    upper = values.astype(jnp.bfloat16)
    lower = (values - upper.astype(jnp.float32)).astype(jnp.bfloat16)
    return (upper, lower)


def times_float(left, right):
    upper, lower = halves(right)
    return dot(left, upper) + dot(left, lower)


def float_times(left, right):
    upper, lower = halves(left)
    return dot(upper, right) + dot(lower, right)


def swap(values, bit, size):
    return lax.ppermute(values, "tensor", [(i, i ^ bit) for i in range(size)])


def gather(values, bits, size):
    for bit in bits:
        values = jnp.concatenate([values, swap(values, bit, size)], axis=0)
    return values


def all_sum(values, bits, size):
    rows, width = values.shape
    block = rows // size
    for place, bit in reversed(list(enumerate(bits))):
        other = swap(values, bit, size).reshape(-1, 2, block << place, width)
        values = values + jnp.flip(other, 1).reshape(rows, width)
    return values


def scatter_sum(values, bits, size):
    for bit in reversed(bits):
        kept, sent = jnp.split(values, 2, axis=0)
        values = kept + swap(sent.astype(jnp.bfloat16), bit, size).astype(jnp.float32)
    return values


def shards(size, rows_in, grad_out, w_gate, w_up, w_down, a_gate, b_gate, a_up, b_up, a_down, b_down):
    bits = []
    while 1 << len(bits) < size:
        bits.insert(0, 1 << len(bits))
    width = a_gate.shape[0]
    own = rows_in.shape[0]
    both = gather(jnp.stack([rows_in, grad_out])[None], bits, size)
    whole_x = both[:, 0].reshape(size * own, -1)
    whole_dy = both[:, 1].reshape(size * own, -1)
    first_col = lax.axis_index("tensor") * width
    x_cols = lax.dynamic_slice_in_dim(whole_x, first_col, width, 1)
    dy_cols = lax.dynamic_slice_in_dim(whole_dy, first_col, width, 1)
    parts = jnp.concatenate([dot(x_cols, a_gate), dot(x_cols, a_up), dot(dy_cols, b_down.T)], axis=1)
    lat_gate, lat_up, back = jnp.split(all_sum(parts, bits, size).astype(jnp.bfloat16), 3, axis=1)
    gate_pre = dot(whole_x, w_gate) + dot(lat_gate, b_gate)
    up_pre = dot(whole_x, w_up) + dot(lat_up, b_up)
    sigma = jax.nn.sigmoid(gate_pre)
    act = gate_pre * sigma
    hidden = (act * up_pre).astype(jnp.bfloat16)
    grad_hidden = dot(whole_dy, w_down.T) + dot(back, a_down.T)
    grad_a_down = dot(hidden.T, back)
    d_up = (grad_hidden * act).astype(jnp.bfloat16)
    d_gate = (grad_hidden * up_pre * sigma * (1.0 + gate_pre * (1.0 - sigma))).astype(jnp.bfloat16)
    grad_b_up = dot(lat_up.T, d_up)
    grad_b_gate = dot(lat_gate.T, d_gate)
    parts = jnp.concatenate([dot(d_up, b_up.T), dot(d_gate, b_gate.T), dot(hidden, a_down)], axis=1)
    t_up, t_gate, lat_down = jnp.split(all_sum(parts, bits, size), 3, axis=1)
    grad_b_down = dot(lat_down.astype(jnp.bfloat16).T, dy_cols)
    grad_a_gate = times_float(x_cols.T, t_gate)
    grad_a_up = times_float(x_cols.T, t_up)
    partial = dot(d_gate, w_gate.T) + dot(d_up, w_up.T)
    adapter = float_times(t_gate, a_gate.T) + float_times(t_up, a_up.T)
    adapter = adapter + lax.dynamic_slice_in_dim(partial, first_col, width, 1)
    partial = lax.dynamic_update_slice_in_dim(partial, adapter, first_col, 1)
    grad_rows = scatter_sum(partial, bits, size)
    return (grad_rows, grad_a_gate, grad_b_gate, grad_a_up, grad_b_up, grad_a_down, grad_b_down)


def solution(mesh):
    size = mesh.shape["tensor"]
    rows, cols, split = P(("groups", "tensor"), None), P(None, "tensor"), P("tensor", None)
    in_specs = (rows, rows, cols, cols, split, split, cols, split, cols, split, cols)
    out_specs = (rows, rows, P("groups", "tensor"), rows, P("groups", "tensor"), rows, P("groups", "tensor"))

    def whole(*arrays):
        return shards(size, *arrays)

    return jax.shard_map(whole, mesh=mesh, in_specs=in_specs, out_specs=out_specs, check_vma=False)
```

```python
import functools

import jax
import jax.numpy as jnp
from jax import lax
from jax.experimental import pallas as pl
from jax.experimental.pallas import tpu as pltpu
from jax.sharding import PartitionSpec as P

F32, BF16 = jnp.float32, jnp.bfloat16
NT, TN = (((1,), (1,)), ((), ())), (((0,), (0,)), ((), ()))
RANK, LANES, STRIP, AHEAD = 64, 128, 512, 4
VMEM = pl.BlockSpec(memory_space=pltpu.VMEM)
SMEM = pl.BlockSpec(memory_space=pltpu.SMEM)
HBM = pl.BlockSpec(memory_space=pltpu.HBM)


def dot(left, right, dims=(((1,), (0,)), ((), ()))):
    return lax.dot_general(left, right, dims, preferred_element_type=F32)


def halves(values):
    upper = values.astype(BF16)
    return upper, (values - upper.astype(F32)).astype(BF16)


def swap(values, flip, size):
    return lax.ppermute(values, "tensor", [(i, i ^ flip) for i in range(size)])


def place_flips(size):
    return [size >> k for k in range(1, size.bit_length())]


def spread(block, size):
    first, second = place_flips(size)[:2]
    return [swap(block, flip, size) for flip in (first, second, first | second)]


def gather(held, size):
    flips = place_flips(size)
    for flip in flips[2:-2]:
        held = jnp.concatenate([held, swap(held, flip, size)])
    return held, swap(held, flips[-2], size)


def reordered(values, block, mask):
    return jnp.concatenate([values[(k ^ mask) * block : (k ^ mask) * block + block] for k in range(values.shape[0] // block)])


def window(start, width, whole):
    span = min(whole, -(-(width + LANES - 1) // LANES) * LANES)
    base = jnp.minimum(start // LANES * LANES, whole - span)
    return pl.ds(pl.multiple_of(base, LANES), span), span, start - base


def block_window(size, me, block, width, whole):
    flips = place_flips(size)[2:]
    return window((me ^ sum(flip * (block >> k & 1) for k, flip in enumerate(flips))) * width, width, whole)


def cut(values, span, shift, width):
    return pltpu.roll(values, lax.rem(span - shift, span), 1)[:, :width].astype(BF16)


def pack(rows_in, grad_out, a_gate, a_up, b_down, both, adapter, rows_s, grad_s, arrived):
    targets = [rows_s, grad_s] + [adapter.at[pl.ds(k * RANK, RANK)] for k in range(3)]
    sources = (rows_in, grad_out, a_gate, a_up, b_down)
    copies = [pltpu.make_async_copy(s, t, arrived.at[k]) for k, (s, t) in enumerate(zip(sources, targets))]
    for copy in copies:
        copy.start()
    for copy in copies:
        copy.wait()
    both[...] = jnp.concatenate([rows_s[...].astype(F32), grad_s[...].astype(F32)]).astype(BF16)


def stack(size, index, *refs):
    blocks, adapters, (held, out) = refs[:4], refs[4:-2], refs[-2:]
    rows, depth = blocks[0].shape
    own, width = rows // 2, adapters[0].shape[1]
    for k, block in enumerate(blocks):
        held[k] = block[...]
    lats, back = jnp.zeros((4 * own, 2 * RANK), F32), jnp.zeros((4 * own, RANK), F32)
    for block, adapter in enumerate(adapters):
        columns, span, shift = block_window(size, index[0], block, width, depth)
        taken = [held[k, :, columns].astype(F32) for k in range(4)]
        lats += dot(cut(jnp.concatenate([t[:own] for t in taken]), span, shift, width), adapter[: 2 * RANK, :], NT)
        back += dot(cut(jnp.concatenate([t[own:] for t in taken]), span, shift, width), adapter[2 * RANK :, :], NT)
    out[...] = jnp.concatenate([lats, back, jnp.zeros_like(back)], 1)


def latent_sum(own, part, first, second, third, other, out, other_out):
    total = part[...]
    for mask, received in ((1, first), (2, second), (3, third)):
        total += reordered(received[...], own, mask)
    out[...] = total.astype(BF16)
    other_out[...] = other[...]


def layer(size, own, index, *refs):
    sources, factors, rows_refs, lat_refs, refs = refs[:3], refs[3:6], refs[6:10], refs[10:14], refs[14:]
    grad_refs, (kept, small, sent, x_cols, dy_cols), refs = refs[:3], refs[3:8], refs[8:]
    x, dy, w_gate, w_up, w_down, products, narrow, grads, arrived, narrow_arrived, grads_left = refs
    factor_copies = [pltpu.make_async_copy(f, narrow.at[k], narrow_arrived.at[k]) for k, f in enumerate(factors)]
    grad_copies = [pltpu.make_async_copy(grads.at[k], g, grads_left.at[k]) for k, g in enumerate(grad_refs)]
    strips = [pl.ds(k, min(STRIP, w_down.shape[0] - k)) for k in range(0, w_down.shape[0], STRIP)]
    copies = [
        pltpu.make_async_copy(source.at[strip], target.at[strip], arrived.at[k * len(strips) + j])
        for k, (source, target) in enumerate(zip(sources, (w_gate, w_up, w_down)))
        for j, strip in enumerate(strips)
    ]
    for copy in copies[:AHEAD] + factor_copies:
        copy.start()
    rows, depth = x.shape
    width = x_cols.shape[1]
    quarter, pieces = size // 4, 16 // own
    for group in range(size // pieces):
        places = range(group * pieces, (group + 1) * pieces)
        taken = [rows_refs[p // quarter][p % quarter].astype(F32) for p in places]
        x[pl.ds(group * 16, 16), :] = jnp.concatenate([t[:own] for t in taken]).astype(BF16)
        dy[pl.ds(group * 16, 16), :] = jnp.concatenate([t[own:] for t in taken]).astype(BF16)
    columns, span, shift = window(index[0] * width, width, depth)
    x_cols[...] = cut(x[:, columns].astype(F32), span, shift, width)
    dy_cols[...] = cut(dy[:, columns].astype(F32), span, shift, width)
    lats = jnp.concatenate([lat[...] for lat in lat_refs])
    lat_gate, lat_up, back = (lats[:, k * RANK : (k + 1) * RANK] for k in range(3))
    for k, (left, weight) in enumerate(((x, w_gate), (x, w_up), (dy, w_down))):
        for j, strip in enumerate(strips):
            place = k * len(strips) + j
            copies[place].wait()
            if place + AHEAD < len(copies):
                copies[place + AHEAD].start()
            products[k, :, strip] = dot(left[...], weight[strip, :], NT)
    for copy in factor_copies:
        copy.wait()
    b_gate, b_up, a_down = (narrow[k] for k in range(3))
    gate_pre = products[0] + dot(lat_gate, b_gate)
    up_pre = products[1] + dot(lat_up, b_up)
    grad_hidden = products[2] + dot(back, a_down)
    sigma = jax.nn.sigmoid(gate_pre)
    act = gate_pre * sigma
    hidden = (act * up_pre).astype(BF16)
    d_up = (grad_hidden * act).astype(BF16)
    d_gate = (grad_hidden * up_pre * sigma * (1.0 + gate_pre * (1.0 - sigma))).astype(BF16)
    for k, (left, right) in enumerate(((lat_gate, d_gate), (lat_up, d_up), (back, hidden))):
        grads[k] = dot(left, right, TN)
        grad_copies[k].start()
    sums = jnp.concatenate([dot(d_gate, b_gate, NT), dot(d_up, b_up, NT)], 1)
    lat_down = dot(hidden, a_down, NT)
    half = rows // 2
    lat_down = jnp.concatenate([lat_down[:half], lat_down[half:]], 1)
    small[...] = jnp.concatenate([sums, lat_down])
    for j, part in enumerate([sums[:half], sums[half:], lat_down]):
        sent[:, depth + j * LANES : depth + (j + 1) * LANES] = part.astype(BF16)
    chunk = depth // 5

    def product(step, _):
        columns = pl.ds(pl.multiple_of(step * chunk, LANES), chunk)
        total = dot(d_gate, w_gate[:, columns]) + dot(d_up, w_up[:, columns])
        kept[:, columns] = total[:half]
        sent[:, columns] = total[half:].astype(BF16)
        return 0

    lax.fori_loop(0, 5, product, 0)
    for copy in grad_copies:
        copy.wait()


def split(total, kept, sent):
    left = kept.shape[0]
    kept[...] = total[:left]
    sent[...] = total[left:].astype(BF16)


def fold_core(kept, small, received, kept_out, sent, small_out, small_sent):
    depth = kept.shape[1]
    split(kept[...] + received[:, :depth].astype(F32), kept_out, sent)
    parts = [received[:, depth + k * LANES : depth + (k + 1) * LANES].astype(F32) for k in range(3)]
    total = small[...] + jnp.concatenate([parts[1], parts[0], pltpu.roll(parts[2], RANK, 1)])
    small_out[...] = total
    small_sent[...] = total.astype(BF16)


def fold(kept, received, kept_out, sent):
    split(kept[...] + received[...].astype(F32), kept_out, sent)


def fold_small(block, masks, small, *refs):
    received, (small_out, small_sent) = refs[: len(masks)], refs[len(masks) :]
    total = small[...]
    for mask, values in zip(masks, received):
        total += reordered(values[...].astype(F32), block, mask)
    small_out[...] = total
    small_sent[...] = total.astype(BF16)


def fold_adapters(size, index, kept, received, small, *refs):
    adapters, (kept_out, sent, total) = refs[:-3], refs[-3:]
    rows, depth = kept.shape
    width = adapters[0].shape[1]
    total[...] = kept[...] + received[...].astype(F32)
    upper, lower = halves(small[:rows])
    for block, adapter in enumerate(adapters):
        columns, span, shift = block_window(size, index[0], block, width, depth)
        part = dot(upper, adapter[: 2 * RANK, :]) + dot(lower, adapter[: 2 * RANK, :])
        part = jnp.concatenate([part, jnp.zeros((rows, span - width), F32)], 1)
        total[:, columns] += pltpu.roll(part, shift, 1)
    split(total[...], kept_out, sent)


def finish_rows(kept, received, out):
    out[...] = kept[...] + received[...].astype(F32)


def finish_small(small, x_cols, dy_cols, grad_a_gate, grad_a_up, grad_b_down):
    rows = x_cols.shape[0]
    upper, lower = halves(small[:rows])
    grads = dot(upper, x_cols[...], TN) + dot(lower, x_cols[...], TN)
    grad_a_gate[...] = grads[:RANK]
    grad_a_up[...] = grads[RANK:]
    lat_down = small[rows:].astype(BF16)
    half = rows // 2
    grad_b_down[...] = dot(lat_down[:, :RANK], dy_cols[:half], TN) + dot(lat_down[:, RANK:], dy_cols[half:], TN)


def call(kernel, inputs, outputs, scratch=(), limit=4 << 20, first=(), first_out=()):
    specs = list(first) + [VMEM] * (len(inputs) - len(first))
    return pl.pallas_call(
        kernel,
        in_specs=specs,
        out_specs=list(first_out) + [VMEM] * (len(outputs) - len(first_out)),
        out_shape=outputs,
        scratch_shapes=scratch,
        compiler_params=pltpu.CompilerParams(vmem_limit_bytes=limit),
    )(*[i if s is SMEM else pltpu.with_memory_space_constraint(i, s.memory_space) for i, s in zip(inputs, specs)])


def shards(size, rows_in, grad_out, w_gate, w_up, w_down, a_gate, b_gate, a_up, b_up, a_down, b_down):
    own, depth = rows_in.shape
    width, hidden = a_gate.shape[0], w_down.shape[0]
    rows = own * size
    flips = place_flips(size)
    out, held = jax.ShapeDtypeStruct, pltpu.VMEM
    index = lax.axis_index("tensor").astype(jnp.int32).reshape(1)

    both, adapter = call(
        pack,
        [rows_in, grad_out, a_gate.T, a_up.T, b_down],
        [held((2 * own, depth), BF16), held((3 * RANK, width), BF16)],
        [held((own, depth), BF16)] * 2 + [pltpu.SemaphoreType.DMA((5,))],
        first=[HBM] * 5,
    )
    blocks = spread(both, size)
    adapters = [adapter]
    for block in range(1, size // 4):
        adapters.append(swap(adapter, sum(flip * (block >> k & 1) for k, flip in enumerate(flips[2:])), size))
    blocks, lats = call(
        functools.partial(stack, size),
        [index, both, *blocks, *adapters],
        [held((4, 2 * own, depth), BF16), held((4 * own, 4 * RANK), F32)],
        first=[SMEM],
    )
    blocks, other = gather(blocks, size)
    lats, other = call(
        functools.partial(latent_sum, own),
        [lats, *spread(lats, size), other],
        [held((4 * own, 4 * RANK), BF16), held(other.shape, BF16)],
    )
    blocks, lats = [blocks, other], gather(lats, size)
    blocks, lats = ([*pair, *(swap(p, flips[-1], size) for p in pair)] for pair in (blocks, lats))

    half, extra = rows // 2, rows // 2 * 3
    small_shape = (extra, 2 * RANK)
    results = call(
        functools.partial(layer, size, own),
        [index, w_gate.T, w_up.T, w_down, b_gate, b_up, a_down.T, *blocks, *lats],
        [pltpu.HBM((RANK, hidden), F32)] * 3
        + [
            held((half, depth), F32),
            held(small_shape, F32),
            held((half, depth + extra // half * LANES), BF16),
            held((rows, width), BF16),
            held((rows, width), BF16),
        ],
        [
            held((rows, depth), BF16),
            held((rows, depth), BF16),
            held((hidden, depth), BF16),
            held((hidden, depth), BF16),
            held((hidden, depth), BF16),
            held((3, rows, hidden), F32),
            held((3, RANK, hidden), BF16),
            held((3, RANK, hidden), F32),
            pltpu.SemaphoreType.DMA((3 * -(-hidden // STRIP),)),
            pltpu.SemaphoreType.DMA((3,)),
            pltpu.SemaphoreType.DMA((3,)),
        ],
        6 * depth * hidden + rows * (130 << 10),
        [SMEM] + [HBM] * 6,
        [HBM] * 3,
    )
    grad_b_gate, grad_b_up, grad_a_down, kept, small, sent, x_cols, dy_cols = results

    def shapes(left):
        return [held((left, depth), F32), held((left, depth), BF16)]

    both_small = [held(small_shape, F32), held(small_shape, BF16)]
    kept, sent, small, small_sent = call(
        fold_core, [kept, small, swap(sent, flips[-1], size)], shapes(half // 2) + both_small
    )
    small, small_sent = call(
        functools.partial(fold_small, own, (1, 2, 3)), [small, *spread(small_sent, size)], both_small
    )
    for k, flip in enumerate(flips[2:-1]):
        small, small_sent = call(
            functools.partial(fold_small, own << k + 2, (1,)), [small, swap(small_sent, flip, size)], both_small
        )
    for flip in reversed(flips[3:-1]):
        kept, sent = call(fold, [kept, swap(sent, flip, size)], shapes(kept.shape[0] // 2))
    kept, sent = call(
        functools.partial(fold_adapters, size),
        [index, kept, swap(sent, flips[2], size), small, *adapters],
        shapes(2 * own),
        [held((4 * own, depth), F32)],
        first=[SMEM],
    )
    kept, sent = call(fold, [kept, swap(sent, flips[1], size)], shapes(own))
    (grad_rows,) = call(finish_rows, [kept, swap(sent, flips[0], size)], [out((own, depth), F32)])
    grad_a_gate, grad_a_up, grad_b_down = call(
        finish_small, [small, x_cols, dy_cols], [out((RANK, width), F32)] * 3
    )
    return (grad_rows, grad_a_gate.T, grad_b_gate, grad_a_up.T, grad_b_up, grad_a_down.T, grad_b_down)


def solution(mesh):
    size = mesh.shape["tensor"]
    rows, cols, split = P(("groups", "tensor"), None), P(None, "tensor"), P("tensor", None)
    in_specs = (rows, rows, cols, cols, split, split, cols, split, cols, split, cols)
    out_specs = (rows, rows, P("groups", "tensor"), rows, P("groups", "tensor"), rows, P("groups", "tensor"))

    def whole(*arrays):
        return shards(size, *arrays)

    return jax.shard_map(whole, mesh=mesh, in_specs=in_specs, out_specs=out_specs, check_vma=False)
```

```python
import functools

import jax
import jax.numpy as jnp
from jax import lax
from jax.experimental import pallas as pl
from jax.experimental.pallas import tpu as pltpu
from jax.sharding import PartitionSpec as P

F32, BF16 = jnp.float32, jnp.bfloat16
NT, TN = (((1,), (1,)), ((), ())), (((0,), (0,)), ((), ()))
RANK, LANES, STRIP = 64, 128, 512
VMEM = pl.BlockSpec(memory_space=pltpu.VMEM)
SMEM = pl.BlockSpec(memory_space=pltpu.SMEM)
HBM = pl.BlockSpec(memory_space=pltpu.HBM)


def dot(left, right, dims=(((1,), (0,)), ((), ()))):
    return lax.dot_general(left, right, dims, preferred_element_type=F32)


def halves(values):
    upper = values.astype(BF16)
    return upper, (values - upper.astype(F32)).astype(BF16)


def swap(values, flip, size):
    return lax.ppermute(values, "tensor", [(i, i ^ flip) for i in range(size)])


def place_flips(size):
    return [size >> k for k in range(1, size.bit_length())]


def spread(block, size):
    first, second = place_flips(size)[:2]
    return [swap(block, flip, size) for flip in (first, second, first | second)]


def gather(held, size):
    flips = place_flips(size)
    for flip in flips[2:-2]:
        held = jnp.concatenate([held, swap(held, flip, size)])
    return held, swap(held, flips[-2], size)


def reordered(values, block, mask):
    return jnp.concatenate([values[(k ^ mask) * block : (k ^ mask) * block + block] for k in range(values.shape[0] // block)])


def window(start, width, whole):
    span = min(whole, -(-(width + LANES - 1) // LANES) * LANES)
    base = jnp.minimum(start // LANES * LANES, whole - span)
    return pl.ds(pl.multiple_of(base, LANES), span), span, start - base


def block_window(size, me, block, width, whole):
    flips = place_flips(size)[2:]
    return window((me ^ sum(flip * (block >> k & 1) for k, flip in enumerate(flips))) * width, width, whole)


def cut(values, span, shift, width):
    return pltpu.roll(values, lax.rem(span - shift, span), 1)[:, :width].astype(BF16)


def pack(rows_in, grad_out, a_gate, a_up, b_down, both, adapter, rows_s, grad_s, arrived):
    targets = [rows_s, grad_s] + [adapter.at[pl.ds(k * RANK, RANK)] for k in range(3)]
    sources = (rows_in, grad_out, a_gate, a_up, b_down)
    copies = [pltpu.make_async_copy(s, t, arrived.at[k]) for k, (s, t) in enumerate(zip(sources, targets))]
    for copy in copies:
        copy.start()
    for copy in copies:
        copy.wait()
    both[...] = jnp.concatenate([rows_s[...].astype(F32), grad_s[...].astype(F32)]).astype(BF16)


def stack(size, index, _, *refs):
    blocks, adapters, (held, out) = refs[:4], refs[4:-2], refs[-2:]
    rows, depth = blocks[0].shape
    own, width = rows // 2, adapters[0].shape[1]
    for k, block in enumerate(blocks):
        held[k] = block[...]
    lats, back = jnp.zeros((4 * own, 2 * RANK), F32), jnp.zeros((4 * own, RANK), F32)
    for block, adapter in enumerate(adapters):
        columns, span, shift = block_window(size, index[0], block, width, depth)
        taken = [held[k, :, columns].astype(F32) for k in range(4)]
        lats += dot(cut(jnp.concatenate([t[:own] for t in taken]), span, shift, width), adapter[: 2 * RANK, :], NT)
        back += dot(cut(jnp.concatenate([t[own:] for t in taken]), span, shift, width), adapter[2 * RANK :, :], NT)
    out[...] = jnp.concatenate([lats, back, jnp.zeros_like(back)], 1)


def load(_, weight, weight_out, done, arrived):
    done[...] = jnp.zeros_like(done)
    copy = pltpu.make_async_copy(weight, weight_out, arrived)
    copy.start()
    copy.wait()


def latent_sum(own, part, first, second, third, other, out, other_out):
    total = part[...]
    for mask, received in ((1, first), (2, second), (3, third)):
        total += reordered(received[...], own, mask)
    out[...] = total.astype(BF16)
    other_out[...] = other[...]


def first_product(size, own, index, source, *refs):
    rows_refs, (x, product, x_cols, dy_cols, weight, dy, arrived) = refs[:4], refs[4:]
    strips = strips_of(weight.shape[0])
    copies = [pltpu.make_async_copy(source.at[s], weight.at[s], arrived.at[j]) for j, s in enumerate(strips)]
    for copy in copies:
        copy.start()
    depth = x.shape[1]
    width = x_cols.shape[1]
    quarter, pieces = size // 4, 16 // own
    for group in range(size // pieces):
        places = range(group * pieces, (group + 1) * pieces)
        taken = [rows_refs[p // quarter][p % quarter].astype(F32) for p in places]
        x[pl.ds(group * 16, 16), :] = jnp.concatenate([t[:own] for t in taken]).astype(BF16)
        dy[pl.ds(group * 16, 16), :] = jnp.concatenate([t[own:] for t in taken]).astype(BF16)
    columns, span, shift = window(index[0] * width, width, depth)
    x_cols[...] = cut(x[:, columns].astype(F32), span, shift, width)
    dy_cols[...] = cut(dy[:, columns].astype(F32), span, shift, width)
    for copy, strip in zip(copies, strips):
        copy.wait()
        product[:, strip] = dot(dy[...], weight[strip, :], NT)


def strips_of(hidden):
    return [pl.ds(k, min(STRIP, hidden - k)) for k in range(0, hidden, STRIP)]


def layer(source, *refs):
    factors, lat_refs, (x, hidden_raw, w_up), refs = refs[:3], refs[3:7], refs[7:10], refs[10:]
    grad_refs, (kept, small, sent), refs = refs[:3], refs[3:6], refs[6:]
    w_gate, gate_raw, up_raw, narrow, grads, arrived, narrow_arrived, grads_left = refs
    factor_copies = [pltpu.make_async_copy(f, narrow.at[k], narrow_arrived.at[k]) for k, f in enumerate(factors)]
    grad_copies = [pltpu.make_async_copy(grads.at[k], g, grads_left.at[k]) for k, g in enumerate(grad_refs)]
    strips = strips_of(w_gate.shape[0])
    copies = [pltpu.make_async_copy(source.at[s], w_gate.at[s], arrived.at[j]) for j, s in enumerate(strips)]
    for copy in copies + factor_copies:
        copy.start()
    rows, depth = x.shape
    lats = jnp.concatenate([lat[...] for lat in lat_refs])
    lat_gate, lat_up, back = (lats[:, k * RANK : (k + 1) * RANK] for k in range(3))
    for strip in strips:
        up_raw[:, strip] = dot(x[...], w_up[strip, :], NT)
    for copy, strip in zip(copies, strips):
        copy.wait()
        gate_raw[:, strip] = dot(x[...], w_gate[strip, :], NT)
    for copy in factor_copies:
        copy.wait()
    b_gate, b_up, a_down = (narrow[k] for k in range(3))
    gate_pre = gate_raw[...] + dot(lat_gate, b_gate)
    up_pre = up_raw[...] + dot(lat_up, b_up)
    grad_hidden = hidden_raw[...] + dot(back, a_down)
    sigma = jax.nn.sigmoid(gate_pre)
    act = gate_pre * sigma
    hidden = (act * up_pre).astype(BF16)
    d_up = (grad_hidden * act).astype(BF16)
    d_gate = (grad_hidden * up_pre * sigma * (1.0 + gate_pre * (1.0 - sigma))).astype(BF16)
    for k, (left, right) in enumerate(((lat_gate, d_gate), (lat_up, d_up), (back, hidden))):
        grads[k] = dot(left, right, TN)
        grad_copies[k].start()
    sums = jnp.concatenate([dot(d_gate, b_gate, NT), dot(d_up, b_up, NT)], 1)
    lat_down = dot(hidden, a_down, NT)
    half = rows // 2
    lat_down = jnp.concatenate([lat_down[:half], lat_down[half:]], 1)
    small[...] = jnp.concatenate([sums, lat_down])
    for j, part in enumerate([sums[:half], sums[half:], lat_down]):
        sent[:, depth + j * LANES : depth + (j + 1) * LANES] = part.astype(BF16)
    chunk = depth // 5

    def product(step, _):
        columns = pl.ds(pl.multiple_of(step * chunk, LANES), chunk)
        total = dot(d_gate, w_gate[:, columns]) + dot(d_up, w_up[:, columns])
        kept[:, columns] = total[:half]
        sent[:, columns] = total[half:].astype(BF16)
        return 0

    lax.fori_loop(0, 5, product, 0)
    for copy in grad_copies:
        copy.wait()


def split(total, kept, sent):
    left = kept.shape[0]
    kept[...] = total[:left]
    sent[...] = total[left:].astype(BF16)


def fold_core(kept, small, received, kept_out, sent, small_out, small_sent):
    depth = kept.shape[1]
    split(kept[...] + received[:, :depth].astype(F32), kept_out, sent)
    parts = [received[:, depth + k * LANES : depth + (k + 1) * LANES].astype(F32) for k in range(3)]
    total = small[...] + jnp.concatenate([parts[1], parts[0], pltpu.roll(parts[2], RANK, 1)])
    small_out[...] = total
    small_sent[...] = total.astype(BF16)


def fold(kept, received, kept_out, sent):
    split(kept[...] + received[...].astype(F32), kept_out, sent)


def fold_small(block, masks, small, *refs):
    received, (small_out, small_sent) = refs[: len(masks)], refs[len(masks) :]
    total = small[...]
    for mask, values in zip(masks, received):
        total += reordered(values[...].astype(F32), block, mask)
    small_out[...] = total
    small_sent[...] = total.astype(BF16)


def fold_adapters(size, block, index, kept, received, small, received_small, *refs):
    adapters, (kept_out, sent, small_out, total) = refs[:-4], refs[-4:]
    small_out[...] = small[...] + reordered(received_small[...].astype(F32), block, 1)
    rows, depth = kept.shape
    width = adapters[0].shape[1]
    total[...] = kept[...] + received[...].astype(F32)
    upper, lower = halves(small_out[:rows])
    for block, adapter in enumerate(adapters):
        columns, span, shift = block_window(size, index[0], block, width, depth)
        part = dot(upper, adapter[: 2 * RANK, :]) + dot(lower, adapter[: 2 * RANK, :])
        part = jnp.concatenate([part, jnp.zeros((rows, span - width), F32)], 1)
        total[:, columns] += pltpu.roll(part, shift, 1)
    split(total[...], kept_out, sent)


def finish_rows(kept, received, out):
    out[...] = kept[...] + received[...].astype(F32)


def finish_small(_, small, x_cols, dy_cols, grad_a_gate, grad_a_up, grad_b_down):
    rows = x_cols.shape[0]
    upper, lower = halves(small[:rows])
    grads = dot(upper, x_cols[...], TN) + dot(lower, x_cols[...], TN)
    grad_a_gate[...] = grads[:RANK]
    grad_a_up[...] = grads[RANK:]
    lat_down = small[rows:].astype(BF16)
    half = rows // 2
    grad_b_down[...] = dot(lat_down[:, :RANK], dy_cols[:half], TN) + dot(lat_down[:, RANK:], dy_cols[half:], TN)


def call(kernel, inputs, outputs, scratch=(), limit=4 << 20, first=(), first_out=(), cost=None):
    specs = list(first) + [VMEM] * (len(inputs) - len(first))
    return pl.pallas_call(
        kernel,
        in_specs=specs,
        out_specs=list(first_out) + [VMEM] * (len(outputs) - len(first_out)),
        out_shape=outputs,
        scratch_shapes=scratch,
        cost_estimate=cost,
        compiler_params=pltpu.CompilerParams(vmem_limit_bytes=limit),
    )(*[i if s is SMEM else pltpu.with_memory_space_constraint(i, s.memory_space) for i, s in zip(inputs, specs)])


def shards(size, rows_in, grad_out, w_gate, w_up, w_down, a_gate, b_gate, a_up, b_up, a_down, b_down):
    own, depth = rows_in.shape
    width, hidden = a_gate.shape[0], w_down.shape[0]
    rows = own * size
    flips = place_flips(size)
    out, held = jax.ShapeDtypeStruct, pltpu.VMEM
    index = lax.axis_index("tensor").astype(jnp.int32).reshape(1)

    both, adapter = call(
        pack,
        [rows_in, grad_out, a_gate.T, a_up.T, b_down],
        [held((2 * own, depth), BF16), held((3 * RANK, width), BF16)],
        [held((own, depth), BF16)] * 2 + [pltpu.SemaphoreType.DMA((5,))],
        first=[HBM] * 5,
    )
    up_in, loaded = call(
        load, [both, w_up.T], [held((hidden, depth), BF16), held((8, LANES), F32)], [pltpu.SemaphoreType.DMA(())], first=[VMEM, HBM]
    )
    blocks = spread(both, size)
    adapters = [adapter]
    for block in range(1, size // 4):
        adapters.append(swap(adapter, sum(flip * (block >> k & 1) for k, flip in enumerate(flips[2:])), size))
    blocks, lats = call(
        functools.partial(stack, size),
        [index, loaded, both, *blocks, *adapters],
        [held((4, 2 * own, depth), BF16), held((4 * own, 4 * RANK), F32)],
        first=[SMEM],
    )
    blocks, other = gather(blocks, size)
    lats, other = call(
        functools.partial(latent_sum, own),
        [lats, *spread(lats, size), other],
        [held((4 * own, 4 * RANK), BF16), held(other.shape, BF16)],
    )
    blocks = [blocks, other, swap(blocks, flips[-1], size), swap(other, flips[-1], size)]
    for flip in flips[2:-2]:
        lats = jnp.concatenate([lats, swap(lats, flip, size)])
    lats = [lats] + [swap(lats, flip, size) for flip in (flips[-2], flips[-1], flips[-2] | flips[-1])]

    half, extra = rows // 2, rows // 2 * 3
    small_shape = (extra, 2 * RANK)
    weight, product = held((hidden, depth), BF16), held((rows, hidden), F32)
    x, hidden_raw, x_cols, dy_cols = call(
        functools.partial(first_product, size, own),
        [index, w_down, *blocks],
        [held((rows, depth), BF16), product, held((rows, width), BF16), held((rows, width), BF16)],
        [weight, held((rows, depth), BF16), pltpu.SemaphoreType.DMA((-(-hidden // STRIP),))],
        2 * depth * hidden + rows * (80 << 10),
        [SMEM, HBM],
        cost=pl.CostEstimate(flops=2 * rows * depth * hidden, transcendentals=0, bytes_accessed=2 * depth * hidden),
    )
    grad_b_gate, grad_b_up, grad_a_down, kept, small, sent = call(
        layer,
        [w_gate.T, b_gate, b_up, a_down.T, *lats, x, hidden_raw, up_in],
        [pltpu.HBM((RANK, hidden), F32)] * 3
        + [held((half, depth), F32), held(small_shape, F32), held((half, depth + extra // half * LANES), BF16)],
        [
            weight,
            product,
            product,
            held((3, RANK, hidden), BF16),
            held((3, RANK, hidden), F32),
            pltpu.SemaphoreType.DMA((-(-hidden // STRIP),)),
            pltpu.SemaphoreType.DMA((3,)),
            pltpu.SemaphoreType.DMA((3,)),
        ],
        2 * depth * hidden + rows * (110 << 10),
        [HBM] * 4,
        [HBM] * 3,
    )

    def shapes(left):
        return [held((left, depth), F32), held((left, depth), BF16)]

    both_small = [held(small_shape, F32), held(small_shape, BF16)]
    kept, sent, small, small_sent = call(
        fold_core, [kept, small, swap(sent, flips[-1], size)], shapes(half // 2) + both_small
    )
    small, small_sent = call(
        functools.partial(fold_small, own, (1, 2, 3)), [small, *spread(small_sent, size)], both_small
    )
    for k, flip in enumerate(flips[2:-2]):
        small, small_sent = call(
            functools.partial(fold_small, own << k + 2, (1,)), [small, swap(small_sent, flip, size)], both_small
        )
    for flip in reversed(flips[3:-1]):
        kept, sent = call(fold, [kept, swap(sent, flip, size)], shapes(kept.shape[0] // 2))
    kept, sent, small = call(
        functools.partial(fold_adapters, size, rows // 4),
        [index, kept, swap(sent, flips[2], size), small, swap(small_sent, flips[-2], size), *adapters],
        shapes(2 * own) + both_small[:1],
        [held((4 * own, depth), F32)],
        first=[SMEM],
    )
    grad_a_gate, grad_a_up, grad_b_down = call(
        finish_small, [kept, small, x_cols, dy_cols], [out((RANK, width), F32)] * 3
    )
    kept, sent = call(fold, [kept, swap(sent, flips[1], size)], shapes(own))
    (grad_rows,) = call(finish_rows, [kept, swap(sent, flips[0], size)], [out((own, depth), F32)])
    return (grad_rows, grad_a_gate.T, grad_b_gate, grad_a_up.T, grad_b_up, grad_a_down.T, grad_b_down)


def solution(mesh):
    size = mesh.shape["tensor"]
    rows, cols, split = P(("groups", "tensor"), None), P(None, "tensor"), P("tensor", None)
    in_specs = (rows, rows, cols, cols, split, split, cols, split, cols, split, cols)
    out_specs = (rows, rows, P("groups", "tensor"), rows, P("groups", "tensor"), rows, P("groups", "tensor"))

    def whole(*arrays):
        return shards(size, *arrays)

    return jax.shard_map(whole, mesh=mesh, in_specs=in_specs, out_specs=out_specs, check_vma=False)
```

```python
import functools

import jax
import jax.numpy as jnp
from jax import lax
from jax.experimental import pallas as pl
from jax.experimental.pallas import tpu as pltpu
from jax.sharding import PartitionSpec as P

F32, BF16 = jnp.float32, jnp.bfloat16
NT, TN = (((1,), (1,)), ((), ())), (((0,), (0,)), ((), ()))
RANK, LANES, STRIP = 64, 128, 512
VMEM = pl.BlockSpec(memory_space=pltpu.VMEM)
SMEM = pl.BlockSpec(memory_space=pltpu.SMEM)
HBM = pl.BlockSpec(memory_space=pltpu.HBM)


def dot(left, right, dims=(((1,), (0,)), ((), ()))):
    return lax.dot_general(left, right, dims, preferred_element_type=F32)


def halves(values):
    upper = values.astype(BF16)
    return upper, (values - upper.astype(F32)).astype(BF16)


def swap(values, flip, size):
    return lax.ppermute(values, "tensor", [(i, i ^ flip) for i in range(size)])


def place_flips(size):
    return [size >> k for k in range(1, size.bit_length())]


def spread(block, size):
    first, second = place_flips(size)[:2]
    return [swap(block, flip, size) for flip in (first, second, first | second)]


def gather(held, size):
    flips = place_flips(size)
    for flip in flips[2:-2]:
        held = jnp.concatenate([held, swap(held, flip, size)])
    return held, swap(held, flips[-2], size)


def reordered(values, block, mask):
    return jnp.concatenate([values[(k ^ mask) * block : (k ^ mask) * block + block] for k in range(values.shape[0] // block)])


def window(start, width, whole):
    span = min(whole, -(-(width + LANES - 1) // LANES) * LANES)
    base = jnp.minimum(start // LANES * LANES, whole - span)
    return pl.ds(pl.multiple_of(base, LANES), span), span, start - base


def block_window(size, me, block, width, whole):
    flips = place_flips(size)[2:]
    return window((me ^ sum(flip * (block >> k & 1) for k, flip in enumerate(flips))) * width, width, whole)


def cut(values, span, shift, width):
    return pltpu.roll(values, lax.rem(span - shift, span), 1)[:, :width].astype(BF16)


def pack(rows_in, grad_out, a_gate, a_up, b_down, both, adapter, rows_s, grad_s, arrived):
    targets = [rows_s, grad_s] + [adapter.at[pl.ds(k * RANK, RANK)] for k in range(3)]
    sources = (rows_in, grad_out, a_gate, a_up, b_down)
    copies = [pltpu.make_async_copy(s, t, arrived.at[k]) for k, (s, t) in enumerate(zip(sources, targets))]
    for copy in copies:
        copy.start()
    for copy in copies:
        copy.wait()
    both[...] = jnp.concatenate([rows_s[...].astype(F32), grad_s[...].astype(F32)]).astype(BF16)


def stack(size, index, _, *refs):
    blocks, adapters, (held, out) = refs[:4], refs[4:-2], refs[-2:]
    rows, depth = blocks[0].shape
    own, width = rows // 2, adapters[0].shape[1]
    for k, block in enumerate(blocks):
        held[k] = block[...]
    lats, back = jnp.zeros((4 * own, 2 * RANK), F32), jnp.zeros((4 * own, RANK), F32)
    for block, adapter in enumerate(adapters):
        columns, span, shift = block_window(size, index[0], block, width, depth)
        taken = [held[k, :, columns].astype(F32) for k in range(4)]
        lats += dot(cut(jnp.concatenate([t[:own] for t in taken]), span, shift, width), adapter[: 2 * RANK, :], NT)
        back += dot(cut(jnp.concatenate([t[own:] for t in taken]), span, shift, width), adapter[2 * RANK :, :], NT)
    out[...] = jnp.concatenate([lats, back, jnp.zeros_like(back)], 1)


def load(_, weight, weight_out, done, arrived):
    done[...] = jnp.zeros_like(done)
    copy = pltpu.make_async_copy(weight, weight_out, arrived)
    copy.start()
    copy.wait()


def latent_sum(own, part, first, second, third, other, out, other_out):
    total = part[...]
    for mask, received in ((1, first), (2, second), (3, third)):
        total += reordered(received[...], own, mask)
    out[...] = total.astype(BF16)
    other_out[...] = other[...]


def first_product(size, own, index, source, *refs):
    rows_refs, (x, product, x_cols, dy_cols, weight, dy, arrived) = refs[:4], refs[4:]
    strips = strips_of(weight.shape[0])
    copies = [pltpu.make_async_copy(source.at[s], weight.at[s], arrived.at[j]) for j, s in enumerate(strips)]
    for copy in copies:
        copy.start()
    depth = x.shape[1]
    width = x_cols.shape[1]
    quarter, pieces = size // 4, 16 // own
    for group in range(size // pieces):
        places = range(group * pieces, (group + 1) * pieces)
        taken = [rows_refs[p // quarter][p % quarter].astype(F32) for p in places]
        x[pl.ds(group * 16, 16), :] = jnp.concatenate([t[:own] for t in taken]).astype(BF16)
        dy[pl.ds(group * 16, 16), :] = jnp.concatenate([t[own:] for t in taken]).astype(BF16)
    columns, span, shift = window(index[0] * width, width, depth)
    x_cols[...] = cut(x[:, columns].astype(F32), span, shift, width)
    dy_cols[...] = cut(dy[:, columns].astype(F32), span, shift, width)
    for copy, strip in zip(copies, strips):
        copy.wait()
        product[:, strip] = dot(dy[...], weight[strip, :], NT)


def strips_of(hidden):
    return [pl.ds(k, min(STRIP, hidden - k)) for k in range(0, hidden, STRIP)]


def layer(source, *refs):
    factors, lat_refs, (x, hidden_raw, w_up), refs = refs[:3], refs[3:7], refs[7:10], refs[10:]
    grad_refs, (kept, small, sent), refs = refs[:3], refs[3:6], refs[6:]
    w_gate, gate_raw, up_raw, narrow, grads, arrived, narrow_arrived, grads_left = refs
    factor_copies = [pltpu.make_async_copy(f, narrow.at[k], narrow_arrived.at[k]) for k, f in enumerate(factors)]
    grad_copies = [pltpu.make_async_copy(grads.at[k], g, grads_left.at[k]) for k, g in enumerate(grad_refs)]
    strips = strips_of(w_gate.shape[0])
    copies = [pltpu.make_async_copy(source.at[s], w_gate.at[s], arrived.at[j]) for j, s in enumerate(strips)]
    for copy in copies + factor_copies:
        copy.start()
    rows, depth = x.shape
    lats = jnp.concatenate([lat[...] for lat in lat_refs])
    lat_gate, lat_up, back = (lats[:, k * RANK : (k + 1) * RANK] for k in range(3))
    for strip in strips:
        up_raw[:, strip] = dot(x[...], w_up[strip, :], NT)
    for copy, strip in zip(copies, strips):
        copy.wait()
        gate_raw[:, strip] = dot(x[...], w_gate[strip, :], NT)
    for copy in factor_copies:
        copy.wait()
    b_gate, b_up, a_down = (narrow[k] for k in range(3))
    gate_pre = gate_raw[...] + dot(lat_gate, b_gate)
    up_pre = up_raw[...] + dot(lat_up, b_up)
    grad_hidden = hidden_raw[...] + dot(back, a_down)
    sigma = jax.nn.sigmoid(gate_pre)
    act = gate_pre * sigma
    hidden = (act * up_pre).astype(BF16)
    d_up = (grad_hidden * act).astype(BF16)
    d_gate = (grad_hidden * up_pre * sigma * (1.0 + gate_pre * (1.0 - sigma))).astype(BF16)
    for k, (left, right) in enumerate(((lat_gate, d_gate), (lat_up, d_up), (back, hidden))):
        grads[k] = dot(left, right, TN)
        grad_copies[k].start()
    sums = jnp.concatenate([dot(d_gate, b_gate, NT), dot(d_up, b_up, NT)], 1)
    lat_down = dot(hidden, a_down, NT)
    half = rows // 2
    lat_down = jnp.concatenate([lat_down[:half], lat_down[half:]], 1)
    small[...] = jnp.concatenate([sums, lat_down])
    for j, part in enumerate([sums[:half], sums[half:], lat_down]):
        sent[:, depth + j * LANES : depth + (j + 1) * LANES] = part.astype(BF16)
    chunk = depth // 5

    def product(step, _):
        columns = pl.ds(pl.multiple_of(step * chunk, LANES), chunk)
        total = dot(d_gate, w_gate[:, columns]) + dot(d_up, w_up[:, columns])
        kept[:, columns] = total[:half]
        sent[:, columns] = total[half:].astype(BF16)
        return 0

    lax.fori_loop(0, 5, product, 0, unroll=True)
    for copy in grad_copies:
        copy.wait()


def split(total, kept, sent):
    left = kept.shape[0]
    kept[...] = total[:left]
    sent[...] = total[left:].astype(BF16)


def fold_core(kept, small, received, kept_out, sent, small_out, small_sent):
    depth = kept.shape[1]
    split(kept[...] + received[:, :depth].astype(F32), kept_out, sent)
    parts = [received[:, depth + k * LANES : depth + (k + 1) * LANES].astype(F32) for k in range(3)]
    total = small[...] + jnp.concatenate([parts[1], parts[0], pltpu.roll(parts[2], RANK, 1)])
    small_out[...] = total
    small_sent[...] = total.astype(BF16)


def fold(kept, received, kept_out, sent):
    split(kept[...] + received[...].astype(F32), kept_out, sent)


def fold_small(block, masks, small, *refs):
    received, (small_out, small_sent) = refs[: len(masks)], refs[len(masks) :]
    total = small[...]
    for mask, values in zip(masks, received):
        total += reordered(values[...].astype(F32), block, mask)
    small_out[...] = total
    small_sent[...] = total.astype(BF16)


def fold_adapters(size, block, index, kept, received, small, received_small, *refs):
    adapters, (kept_out, *sents, small_out, total) = refs[:-6], refs[-6:]
    small_out[...] = small[...] + reordered(received_small[...].astype(F32), block, 1)
    rows, depth = kept.shape
    width = adapters[0].shape[1]
    total[...] = kept[...] + received[...].astype(F32)
    upper, lower = halves(small_out[:rows])
    for block, adapter in enumerate(adapters):
        columns, span, shift = block_window(size, index[0], block, width, depth)
        part = dot(upper, adapter[: 2 * RANK, :]) + dot(lower, adapter[: 2 * RANK, :])
        part = jnp.concatenate([part, jnp.zeros((rows, span - width), F32)], 1)
        total[:, columns] += pltpu.roll(part, shift, 1)
    own = kept_out.shape[0]
    kept_out[...] = total[:own]
    for k, sent in enumerate(sents):
        sent[...] = total[own * (k + 1) : own * (k + 2)].astype(BF16)


def finish_rows(kept, first, second, third, out):
    out[...] = kept[...] + first[...].astype(F32) + second[...].astype(F32) + third[...].astype(F32)


def finish_small(_, small, x_cols, dy_cols, grad_a_gate, grad_a_up, grad_b_down):
    rows = x_cols.shape[0]
    upper, lower = halves(small[:rows])
    grads = dot(upper, x_cols[...], TN) + dot(lower, x_cols[...], TN)
    grad_a_gate[...] = grads[:RANK]
    grad_a_up[...] = grads[RANK:]
    lat_down = small[rows:].astype(BF16)
    half = rows // 2
    grad_b_down[...] = dot(lat_down[:, :RANK], dy_cols[:half], TN) + dot(lat_down[:, RANK:], dy_cols[half:], TN)


def call(kernel, inputs, outputs, scratch=(), limit=4 << 20, first=(), first_out=(), cost=None):
    specs = list(first) + [VMEM] * (len(inputs) - len(first))
    return pl.pallas_call(
        kernel,
        in_specs=specs,
        out_specs=list(first_out) + [VMEM] * (len(outputs) - len(first_out)),
        out_shape=outputs,
        scratch_shapes=scratch,
        cost_estimate=cost,
        compiler_params=pltpu.CompilerParams(vmem_limit_bytes=limit),
    )(*[i if s is SMEM else pltpu.with_memory_space_constraint(i, s.memory_space) for i, s in zip(inputs, specs)])


def shards(size, rows_in, grad_out, w_gate, w_up, w_down, a_gate, b_gate, a_up, b_up, a_down, b_down):
    own, depth = rows_in.shape
    width, hidden = a_gate.shape[0], w_down.shape[0]
    rows = own * size
    flips = place_flips(size)
    out, held = jax.ShapeDtypeStruct, pltpu.VMEM
    index = lax.axis_index("tensor").astype(jnp.int32).reshape(1)

    both, adapter = call(
        pack,
        [rows_in, grad_out, a_gate.T, a_up.T, b_down],
        [held((2 * own, depth), BF16), held((3 * RANK, width), BF16)],
        [held((own, depth), BF16)] * 2 + [pltpu.SemaphoreType.DMA((5,))],
        first=[HBM] * 5,
    )
    up_in, loaded = call(
        load, [both, w_up.T], [held((hidden, depth), BF16), held((8, LANES), F32)], [pltpu.SemaphoreType.DMA(())], first=[VMEM, HBM]
    )
    blocks = spread(both, size)
    adapters = [adapter]
    for block in range(1, size // 4):
        adapters.append(swap(adapter, sum(flip * (block >> k & 1) for k, flip in enumerate(flips[2:])), size))
    blocks, lats = call(
        functools.partial(stack, size),
        [index, loaded, both, *blocks, *adapters],
        [held((4, 2 * own, depth), BF16), held((4 * own, 4 * RANK), F32)],
        first=[SMEM],
    )
    blocks, other = gather(blocks, size)
    lats, other = call(
        functools.partial(latent_sum, own),
        [lats, *spread(lats, size), other],
        [held((4 * own, 4 * RANK), BF16), held(other.shape, BF16)],
    )
    blocks = [blocks, other, swap(blocks, flips[-1], size), swap(other, flips[-1], size)]
    for flip in flips[2:-2]:
        lats = jnp.concatenate([lats, swap(lats, flip, size)])
    lats = [lats] + [swap(lats, flip, size) for flip in (flips[-2], flips[-1], flips[-2] | flips[-1])]

    half, extra = rows // 2, rows // 2 * 3
    small_shape = (extra, 2 * RANK)
    weight, product = held((hidden, depth), BF16), held((rows, hidden), F32)
    x, hidden_raw, x_cols, dy_cols = call(
        functools.partial(first_product, size, own),
        [index, w_down, *blocks],
        [held((rows, depth), BF16), product, held((rows, width), BF16), held((rows, width), BF16)],
        [weight, held((rows, depth), BF16), pltpu.SemaphoreType.DMA((-(-hidden // STRIP),))],
        2 * depth * hidden + rows * (80 << 10),
        [SMEM, HBM],
        cost=pl.CostEstimate(flops=2 * rows * depth * hidden, transcendentals=0, bytes_accessed=2 * depth * hidden),
    )
    grad_b_gate, grad_b_up, grad_a_down, kept, small, sent = call(
        layer,
        [w_gate.T, b_gate, b_up, a_down.T, *lats, x, hidden_raw, up_in],
        [pltpu.HBM((RANK, hidden), F32)] * 3
        + [held((half, depth), F32), held(small_shape, F32), held((half, depth + extra // half * LANES), BF16)],
        [
            weight,
            product,
            product,
            held((3, RANK, hidden), BF16),
            held((3, RANK, hidden), F32),
            pltpu.SemaphoreType.DMA((-(-hidden // STRIP),)),
            pltpu.SemaphoreType.DMA((3,)),
            pltpu.SemaphoreType.DMA((3,)),
        ],
        2 * depth * hidden + rows * (110 << 10),
        [HBM] * 4,
        [HBM] * 3,
    )

    def shapes(left):
        return [held((left, depth), F32), held((left, depth), BF16)]

    both_small = [held(small_shape, F32), held(small_shape, BF16)]
    kept, sent, small, small_sent = call(
        fold_core, [kept, small, swap(sent, flips[-1], size)], shapes(half // 2) + both_small
    )
    small, small_sent = call(
        functools.partial(fold_small, own, (1, 2, 3)), [small, *spread(small_sent, size)], both_small
    )
    for k, flip in enumerate(flips[2:-2]):
        small, small_sent = call(
            functools.partial(fold_small, own << k + 2, (1,)), [small, swap(small_sent, flip, size)], both_small
        )
    for flip in reversed(flips[3:-1]):
        kept, sent = call(fold, [kept, swap(sent, flip, size)], shapes(kept.shape[0] // 2))
    kept, *sents, small = call(
        functools.partial(fold_adapters, size, rows // 4),
        [index, kept, swap(sent, flips[2], size), small, swap(small_sent, flips[-2], size), *adapters],
        [held((own, depth), F32)] + [held((own, depth), BF16)] * 3 + both_small[:1],
        [held((4 * own, depth), F32)],
        first=[SMEM],
    )
    grad_a_gate, grad_a_up, grad_b_down = call(
        finish_small, [kept, small, x_cols, dy_cols], [out((RANK, width), F32)] * 3
    )
    received = [swap(sent, flip, size) for sent, flip in zip(sents, (flips[0], flips[1], flips[0] | flips[1]))]
    (grad_rows,) = call(finish_rows, [kept, *received], [out((own, depth), F32)])
    return (grad_rows, grad_a_gate.T, grad_b_gate, grad_a_up.T, grad_b_up, grad_a_down.T, grad_b_down)


def solution(mesh):
    size = mesh.shape["tensor"]
    rows, cols, split = P(("groups", "tensor"), None), P(None, "tensor"), P("tensor", None)
    in_specs = (rows, rows, cols, cols, split, split, cols, split, cols, split, cols)
    out_specs = (rows, rows, P("groups", "tensor"), rows, P("groups", "tensor"), rows, P("groups", "tensor"))

    def whole(*arrays):
        return shards(size, *arrays)

    return jax.shard_map(whole, mesh=mesh, in_specs=in_specs, out_specs=out_specs, check_vma=False)
```

```python
import functools

import jax
import jax.numpy as jnp
from jax import lax
from jax.experimental import pallas as pl
from jax.experimental.pallas import tpu as pltpu
from jax.sharding import PartitionSpec as P

F32, BF16 = jnp.float32, jnp.bfloat16
NT, TN = (((1,), (1,)), ((), ())), (((0,), (0,)), ((), ()))
RANK, LANES, STRIP = 64, 128, 512
VMEM = pl.BlockSpec(memory_space=pltpu.VMEM)
SMEM = pl.BlockSpec(memory_space=pltpu.SMEM)
HBM = pl.BlockSpec(memory_space=pltpu.HBM)


def dot(left, right, dims=(((1,), (0,)), ((), ()))):
    return lax.dot_general(left, right, dims, preferred_element_type=F32)


def halves(values):
    upper = values.astype(BF16)
    return upper, (values - upper.astype(F32)).astype(BF16)


def swap(values, flip, size):
    return lax.ppermute(values, "tensor", [(i, i ^ flip) for i in range(size)])


def place_flips(size):
    return [size >> k for k in range(1, size.bit_length())]


def spread(block, size):
    first, second = place_flips(size)[:2]
    return [swap(block, flip, size) for flip in (first, second, first | second)]


def gather(held, size):
    flips = place_flips(size)
    for flip in flips[2:-2]:
        held = jnp.concatenate([held, swap(held, flip, size)])
    return held, swap(held, flips[-2], size)


def reordered(values, block, mask):
    return jnp.concatenate([values[(k ^ mask) * block : (k ^ mask) * block + block] for k in range(values.shape[0] // block)])


def window(start, width, whole):
    span = min(whole, -(-(width + LANES - 1) // LANES) * LANES)
    base = jnp.minimum(start // LANES * LANES, whole - span)
    return pl.ds(pl.multiple_of(base, LANES), span), span, start - base


def block_window(size, me, block, width, whole):
    flips = place_flips(size)[2:]
    return window((me ^ sum(flip * (block >> k & 1) for k, flip in enumerate(flips))) * width, width, whole)


def cut(values, span, shift, width):
    return pltpu.roll(values, lax.rem(span - shift, span), 1)[:, :width].astype(BF16)


def pack(rows_in, grad_out, a_gate, a_up, b_down, both, adapter, rows_s, grad_s, arrived):
    targets = [rows_s, grad_s] + [adapter.at[pl.ds(k * RANK, RANK)] for k in range(3)]
    sources = (rows_in, grad_out, a_gate, a_up, b_down)
    copies = [pltpu.make_async_copy(s, t, arrived.at[k]) for k, (s, t) in enumerate(zip(sources, targets))]
    for copy in copies:
        copy.start()
    for copy in copies:
        copy.wait()
    both[...] = jnp.concatenate([rows_s[...].astype(F32), grad_s[...].astype(F32)]).astype(BF16)


def stack(size, index, _, *refs):
    blocks, adapters, (held, out) = refs[:4], refs[4:-2], refs[-2:]
    rows, depth = blocks[0].shape
    own, width = rows // 2, adapters[0].shape[1]
    for k, block in enumerate(blocks):
        held[k] = block[...]
    lats, back = jnp.zeros((4 * own, 2 * RANK), F32), jnp.zeros((4 * own, RANK), F32)
    for block, adapter in enumerate(adapters):
        columns, span, shift = block_window(size, index[0], block, width, depth)
        taken = [held[k, :, columns].astype(F32) for k in range(4)]
        lats += dot(cut(jnp.concatenate([t[:own] for t in taken]), span, shift, width), adapter[: 2 * RANK, :], NT)
        back += dot(cut(jnp.concatenate([t[own:] for t in taken]), span, shift, width), adapter[2 * RANK :, :], NT)
    out[...] = jnp.concatenate([lats, back, jnp.zeros_like(back)], 1)


def load(_, weight, weight_out, done, arrived):
    done[...] = jnp.zeros_like(done)
    copy = pltpu.make_async_copy(weight, weight_out, arrived)
    copy.start()
    copy.wait()


def latent_sum(own, part, first, second, third, other, out, other_out):
    total = part[...]
    for mask, received in ((1, first), (2, second), (3, third)):
        total += reordered(received[...], own, mask)
    out[...] = total.astype(BF16)
    other_out[...] = other[...]


def first_product(size, own, index, source, *refs):
    rows_refs, (x, product, x_cols, dy_cols, weight, dy, arrived) = refs[:4], refs[4:]
    strips = strips_of(weight.shape[0])
    copies = [pltpu.make_async_copy(source.at[s], weight.at[s], arrived.at[j]) for j, s in enumerate(strips)]
    for copy in copies:
        copy.start()
    depth = x.shape[1]
    width = x_cols.shape[1]
    quarter, pieces = size // 4, 16 // own
    for group in range(size // pieces):
        places = range(group * pieces, (group + 1) * pieces)
        taken = [rows_refs[p // quarter][p % quarter].astype(F32) for p in places]
        x[pl.ds(group * 16, 16), :] = jnp.concatenate([t[:own] for t in taken]).astype(BF16)
        dy[pl.ds(group * 16, 16), :] = jnp.concatenate([t[own:] for t in taken]).astype(BF16)
    columns, span, shift = window(index[0] * width, width, depth)
    x_cols[...] = cut(x[:, columns].astype(F32), span, shift, width)
    dy_cols[...] = cut(dy[:, columns].astype(F32), span, shift, width)
    for copy, strip in zip(copies, strips):
        copy.wait()
        product[:, strip] = dot(dy[...], weight[strip, :], NT)


def strips_of(hidden):
    starts = list(range(0, max(hidden - STRIP, 0) + 1, STRIP))
    return [pl.ds(start, end - start) for start, end in zip(starts, [*starts[1:], hidden])]


def layer(source, *refs):
    factors, lat_refs, (x, hidden_raw, w_up), refs = refs[:3], refs[3:7], refs[7:10], refs[10:]
    grad_refs, (kept, small, sent), refs = refs[:3], refs[3:6], refs[6:]
    w_gate, gate_raw, up_raw, narrow, grads, arrived, narrow_arrived, grads_left = refs
    factor_copies = [pltpu.make_async_copy(f, narrow.at[k], narrow_arrived.at[k]) for k, f in enumerate(factors)]
    grad_copies = [pltpu.make_async_copy(grads.at[k], g, grads_left.at[k]) for k, g in enumerate(grad_refs)]
    strips = strips_of(w_gate.shape[0])
    copies = [pltpu.make_async_copy(source.at[s], w_gate.at[s], arrived.at[j]) for j, s in enumerate(strips)]
    for copy in copies + factor_copies:
        copy.start()
    rows, depth = x.shape
    lats = jnp.concatenate([lat[...] for lat in lat_refs])
    lat_gate, lat_up, back = (lats[:, k * RANK : (k + 1) * RANK] for k in range(3))
    for strip in strips:
        up_raw[:, strip] = dot(x[...], w_up[strip, :], NT)
    for copy, strip in zip(copies, strips):
        copy.wait()
        gate_raw[:, strip] = dot(x[...], w_gate[strip, :], NT)
    for copy in factor_copies:
        copy.wait()
    b_gate, b_up, a_down = (narrow[k] for k in range(3))
    gate_pre = gate_raw[...] + dot(lat_gate, b_gate)
    up_pre = up_raw[...] + dot(lat_up, b_up)
    grad_hidden = hidden_raw[...] + dot(back, a_down)
    sigma = jax.nn.sigmoid(gate_pre)
    act = gate_pre * sigma
    hidden = (act * up_pre).astype(BF16)
    d_up = (grad_hidden * act).astype(BF16)
    d_gate = (grad_hidden * up_pre * sigma * (1.0 + gate_pre * (1.0 - sigma))).astype(BF16)
    for k, (left, right) in enumerate(((lat_gate, d_gate), (lat_up, d_up), (back, hidden))):
        grads[k] = dot(left, right, TN)
        grad_copies[k].start()
    sums = jnp.concatenate([dot(d_gate, b_gate, NT), dot(d_up, b_up, NT)], 1)
    lat_down = dot(hidden, a_down, NT)
    half = rows // 2
    lat_down = jnp.concatenate([lat_down[:half], lat_down[half:]], 1)
    small[...] = jnp.concatenate([sums, lat_down])
    for j, part in enumerate([sums[:half], sums[half:], lat_down]):
        sent[:, depth + j * LANES : depth + (j + 1) * LANES] = part.astype(BF16)
    chunk = depth // 5

    def product(step, _):
        columns = pl.ds(pl.multiple_of(step * chunk, LANES), chunk)
        total = dot(d_gate, w_gate[:, columns]) + dot(d_up, w_up[:, columns])
        kept[:, columns] = total[:half]
        sent[:, columns] = total[half:].astype(BF16)
        return 0

    lax.fori_loop(0, 5, product, 0, unroll=True)
    for copy in grad_copies:
        copy.wait()


def split(total, kept, sent):
    left = kept.shape[0]
    kept[...] = total[:left]
    sent[...] = total[left:].astype(BF16)


def fold_core(kept, small, received, kept_out, sent, small_out, small_sent):
    depth = kept.shape[1]
    split(kept[...] + received[:, :depth].astype(F32), kept_out, sent)
    parts = [received[:, depth + k * LANES : depth + (k + 1) * LANES].astype(F32) for k in range(3)]
    total = small[...] + jnp.concatenate([parts[1], parts[0], pltpu.roll(parts[2], RANK, 1)])
    small_out[...] = total
    small_sent[...] = total.astype(BF16)


def fold(kept, received, kept_out, sent):
    split(kept[...] + received[...].astype(F32), kept_out, sent)


def fold_small(block, masks, small, *refs):
    received, (small_out, small_sent) = refs[: len(masks)], refs[len(masks) :]
    total = small[...]
    for mask, values in zip(masks, received):
        total += reordered(values[...].astype(F32), block, mask)
    small_out[...] = total
    small_sent[...] = total.astype(BF16)


def fold_adapters(size, block, index, kept, received, small, received_small, *refs):
    adapters, (kept_out, *sents, small_out, total) = refs[:-6], refs[-6:]
    small_out[...] = small[...] + reordered(received_small[...].astype(F32), block, 1)
    rows, depth = kept.shape
    width = adapters[0].shape[1]
    total[...] = kept[...] + received[...].astype(F32)
    upper, lower = halves(small_out[:rows])
    for block, adapter in enumerate(adapters):
        columns, span, shift = block_window(size, index[0], block, width, depth)
        part = dot(upper, adapter[: 2 * RANK, :]) + dot(lower, adapter[: 2 * RANK, :])
        part = jnp.concatenate([part, jnp.zeros((rows, span - width), F32)], 1)
        total[:, columns] += pltpu.roll(part, shift, 1)
    own = kept_out.shape[0]
    kept_out[...] = total[:own]
    for k, sent in enumerate(sents):
        sent[...] = total[own * (k + 1) : own * (k + 2)].astype(BF16)


def finish_rows(kept, first, second, third, out):
    out[...] = kept[...] + first[...].astype(F32) + second[...].astype(F32) + third[...].astype(F32)


def finish_small(_, small, x_cols, dy_cols, grad_a_gate, grad_a_up, grad_b_down):
    rows = x_cols.shape[0]
    upper, lower = halves(small[:rows])
    grads = dot(upper, x_cols[...], TN) + dot(lower, x_cols[...], TN)
    grad_a_gate[...] = grads[:RANK]
    grad_a_up[...] = grads[RANK:]
    lat_down = small[rows:].astype(BF16)
    half = rows // 2
    grad_b_down[...] = dot(lat_down[:, :RANK], dy_cols[:half], TN) + dot(lat_down[:, RANK:], dy_cols[half:], TN)


def call(kernel, inputs, outputs, scratch=(), limit=4 << 20, first=(), first_out=(), cost=None):
    specs = list(first) + [VMEM] * (len(inputs) - len(first))
    return pl.pallas_call(
        kernel,
        in_specs=specs,
        out_specs=list(first_out) + [VMEM] * (len(outputs) - len(first_out)),
        out_shape=outputs,
        scratch_shapes=scratch,
        cost_estimate=cost,
        compiler_params=pltpu.CompilerParams(vmem_limit_bytes=limit),
    )(*[i if s is SMEM else pltpu.with_memory_space_constraint(i, s.memory_space) for i, s in zip(inputs, specs)])


def shards(size, rows_in, grad_out, w_gate, w_up, w_down, a_gate, b_gate, a_up, b_up, a_down, b_down):
    own, depth = rows_in.shape
    width, hidden = a_gate.shape[0], w_down.shape[0]
    rows = own * size
    flips = place_flips(size)
    out, held = jax.ShapeDtypeStruct, pltpu.VMEM
    index = lax.axis_index("tensor").astype(jnp.int32).reshape(1)

    both, adapter = call(
        pack,
        [rows_in, grad_out, a_gate.T, a_up.T, b_down],
        [held((2 * own, depth), BF16), held((3 * RANK, width), BF16)],
        [held((own, depth), BF16)] * 2 + [pltpu.SemaphoreType.DMA((5,))],
        first=[HBM] * 5,
    )
    up_in, loaded = call(
        load, [both, w_up.T], [held((hidden, depth), BF16), held((8, LANES), F32)], [pltpu.SemaphoreType.DMA(())], first=[VMEM, HBM]
    )
    blocks = spread(both, size)
    adapters = [adapter]
    for block in range(1, size // 4):
        adapters.append(swap(adapter, sum(flip * (block >> k & 1) for k, flip in enumerate(flips[2:])), size))
    blocks, lats = call(
        functools.partial(stack, size),
        [index, loaded, both, *blocks, *adapters],
        [held((4, 2 * own, depth), BF16), held((4 * own, 4 * RANK), F32)],
        first=[SMEM],
    )
    blocks, other = gather(blocks, size)
    lats, other = call(
        functools.partial(latent_sum, own),
        [lats, *spread(lats, size), other],
        [held((4 * own, 4 * RANK), BF16), held(other.shape, BF16)],
    )
    blocks = [blocks, other, swap(blocks, flips[-1], size), swap(other, flips[-1], size)]
    for flip in flips[2:-2]:
        lats = jnp.concatenate([lats, swap(lats, flip, size)])
    lats = [lats] + [swap(lats, flip, size) for flip in (flips[-2], flips[-1], flips[-2] | flips[-1])]

    half, extra = rows // 2, rows // 2 * 3
    small_shape = (extra, 2 * RANK)
    weight, product = held((hidden, depth), BF16), held((rows, hidden), F32)
    x, hidden_raw, x_cols, dy_cols = call(
        functools.partial(first_product, size, own),
        [index, w_down, *blocks],
        [held((rows, depth), BF16), product, held((rows, width), BF16), held((rows, width), BF16)],
        [weight, held((rows, depth), BF16), pltpu.SemaphoreType.DMA((-(-hidden // STRIP),))],
        2 * depth * hidden + rows * (80 << 10),
        [SMEM, HBM],
        cost=pl.CostEstimate(flops=2 * rows * depth * hidden, transcendentals=0, bytes_accessed=2 * depth * hidden),
    )
    grad_b_gate, grad_b_up, grad_a_down, kept, small, sent = call(
        layer,
        [w_gate.T, b_gate, b_up, a_down.T, *lats, x, hidden_raw, up_in],
        [pltpu.HBM((RANK, hidden), F32)] * 3
        + [held((half, depth), F32), held(small_shape, F32), held((half, depth + extra // half * LANES), BF16)],
        [
            weight,
            product,
            product,
            held((3, RANK, hidden), BF16),
            held((3, RANK, hidden), F32),
            pltpu.SemaphoreType.DMA((-(-hidden // STRIP),)),
            pltpu.SemaphoreType.DMA((3,)),
            pltpu.SemaphoreType.DMA((3,)),
        ],
        2 * depth * hidden + rows * (110 << 10),
        [HBM] * 4,
        [HBM] * 3,
    )

    def shapes(left):
        return [held((left, depth), F32), held((left, depth), BF16)]

    both_small = [held(small_shape, F32), held(small_shape, BF16)]
    kept, sent, small, small_sent = call(
        fold_core, [kept, small, swap(sent, flips[-1], size)], shapes(half // 2) + both_small
    )
    small, small_sent = call(
        functools.partial(fold_small, own, (1, 2, 3)), [small, *spread(small_sent, size)], both_small
    )
    for k, flip in enumerate(flips[2:-2]):
        small, small_sent = call(
            functools.partial(fold_small, own << k + 2, (1,)), [small, swap(small_sent, flip, size)], both_small
        )
    for flip in reversed(flips[3:-1]):
        kept, sent = call(fold, [kept, swap(sent, flip, size)], shapes(kept.shape[0] // 2))
    kept, *sents, small = call(
        functools.partial(fold_adapters, size, rows // 4),
        [index, kept, swap(sent, flips[2], size), small, swap(small_sent, flips[-2], size), *adapters],
        [held((own, depth), F32)] + [held((own, depth), BF16)] * 3 + both_small[:1],
        [held((4 * own, depth), F32)],
        first=[SMEM],
    )
    grad_a_gate, grad_a_up, grad_b_down = call(
        finish_small, [kept, small, x_cols, dy_cols], [out((RANK, width), F32)] * 3
    )
    received = [swap(sent, flip, size) for sent, flip in zip(sents, (flips[0], flips[1], flips[0] | flips[1]))]
    (grad_rows,) = call(finish_rows, [kept, *received], [out((own, depth), F32)])
    return (grad_rows, grad_a_gate.T, grad_b_gate, grad_a_up.T, grad_b_up, grad_a_down.T, grad_b_down)


def solution(mesh):
    size = mesh.shape["tensor"]
    rows, cols, split = P(("groups", "tensor"), None), P(None, "tensor"), P("tensor", None)
    in_specs = (rows, rows, cols, cols, split, split, cols, split, cols, split, cols)
    out_specs = (rows, rows, P("groups", "tensor"), rows, P("groups", "tensor"), rows, P("groups", "tensor"))

    def whole(*arrays):
        return shards(size, *arrays)

    return jax.shard_map(whole, mesh=mesh, in_specs=in_specs, out_specs=out_specs, check_vma=False)
```
